32 devices in a mesh: parts: 2 (over x), src: 16 (over z, y, core).
Axes of the slice: x: 2, y: 2, z: 4, core: 2. Of those that a mesh axis runs over, the one named last changes fastest.
Arguments:
- estimate: bfloat16 [64, 32, 1024], P(('parts', 'src')), parts along dimension 0, may hold values from -64 to 64
- records: bfloat16 [8, 32, 1152], P('parts', 'src'), parts along dimension 0, may hold values from -64 to 64
- dip_receiver: bfloat16 [64, 32, 1024], P(('parts', 'src')), parts along dimension 0, may hold values from -1 to 1
- dip_source: bfloat16 [64, 32, 1024], P(('parts', 'src')), parts along dimension 0, may hold values from -1 to 1
- delays: int32 [64], P('parts'), parts along dimension 0, may hold values from 0 to 128
- boat: int32 [64], P('parts'), parts along dimension 0, may hold values from 0 to 3
- pair: int32 [64], P('parts'), parts along dimension 0, may hold values from 0 to 31, as said below
Outputs:
- refined: bfloat16 [64, 32, 1024], P(('parts', 'src')), parts along dimension 0
The draws below stay inside these ranges and needn't reach their ends.
There are 2 independent parts, one for each index of `parts`. The reference program is written for one: setup_inputs(seed, part) draws one part's arguments, and reference() takes and returns one part's arrays. A program takes and returns all parts, laid end to end along the dimension named above; each array names one. Nothing has to cross between parts.
Inputs may be any that keep to these rules, and one draw needn't show every extreme that they name: pair is a permutation that maps each aligned block of 2 indices onto itself.
All inputs are finite; a program needn't handle non-finite values.
Results may differ from the reference program's by a relative error of at most 0.015.
Values may be sent and summed in bfloat16 or wider, within the bound.
A program may use at most 64 MiB of HBM per device.

```python
import jax
import jax.numpy as jnp
from jax import lax

SRC_DEV = 2
NT = 1024
WBLK = 256
DMAX = 128
ITERS = 2
S = 32
R = 32
REC = 4
TB = 1152


def ramp_scale(count):
    return 1.0 + 2.0 * jnp.arange(count, dtype=jnp.float32) / (count - 1)


def draw_estimate(key, part):
    key = jax.random.fold_in(key, 11)
    scale = jnp.sqrt(ramp_scale(S)[:, None, None] * ramp_scale(R)[None, :, None])
    base = jnp.clip(jax.random.normal(key, (S, R, NT), jnp.float32), -6.0, 6.0)
    return (base * scale).astype(jnp.bfloat16)


def draw_records(key, part):
    key = jax.random.fold_in(key, 23)
    scale = 2.0 * jnp.sqrt(ramp_scale(R))[None, :, None]
    base = jnp.clip(jax.random.normal(key, (REC, R, TB), jnp.float32), -6.0, 6.0)
    return (base * scale).astype(jnp.bfloat16)


def draw_pair(key, part):
    key = jax.random.fold_in(key, 37)
    scores = jax.random.randint(key, (S,), 0, 1 << 20) * S + jnp.arange(S, dtype=jnp.int32)
    grouped = scores.reshape(S // SRC_DEV, SRC_DEV)
    order = jnp.argsort(grouped, axis=1, stable=True)
    starts = jnp.arange(0, S, SRC_DEV, dtype=jnp.int32)[:, None]
    return (order.astype(jnp.int32) + starts).reshape(S).astype(jnp.int32)


def set_ends(drawn, stream_key, low, top_value):
    index_at = [jax.random.randint(jax.random.fold_in(stream_key, axis), (), 0, length) for axis, length in enumerate(drawn.shape)]
    widest = drawn.shape.index(max(drawn.shape))
    next_to = index_at[:widest] + [(index_at[widest] + 1) % drawn.shape[widest]] + index_at[widest + 1:]
    return drawn.at[tuple(index_at)].set(low).at[tuple(next_to)].set(top_value)


def shard_levels(stream_key, dims, cuts, low, top_value):
    def one(axis_at, parts):
        heights = jax.random.uniform(jax.random.fold_in(jax.random.fold_in(stream_key, 6), axis_at), (parts,), jnp.float32, low / len(cuts), top_value / len(cuts))
        return jnp.repeat(jnp.exp(heights), dims[axis_at] // parts).reshape((-1,) + (1,) * (len(dims) - axis_at - 1))

    level = one(*cuts[0])
    for cut in cuts[1:]:
        level = level * one(*cut)
    return level


def setup_inputs(seed: int = 0, part: int = 0) -> dict:
    arg_keys = jax.random.split(jax.random.key(seed), 8)
    part_splits = jax.random.split(jax.random.fold_in(arg_keys[7], part), 8)
    estimate = draw_estimate(jax.random.fold_in(jax.random.fold_in(arg_keys[7], part), 71), part)
    records = draw_records(jax.random.fold_in(jax.random.fold_in(arg_keys[7], part), 71), part)
    dip_receiver = jnp.clip(jax.random.uniform(part_splits[2], (S, R, NT), jnp.float32, -1.0, 1.0) * shard_levels(part_splits[2], (S, R, NT), ((0, 16),), -0.4, 0.0), -1.0, 1.0).astype(jnp.bfloat16)
    dip_source = jnp.clip(jax.random.uniform(part_splits[3], (S, R, NT), jnp.float32, -1.0, 1.0) * shard_levels(part_splits[3], (S, R, NT), ((0, 16),), -0.4, 0.0), -1.0, 1.0).astype(jnp.bfloat16)
    delays = set_ends(jax.random.randint(part_splits[4], (S,), 0, DMAX + 1), jax.random.fold_in(part_splits[4], 1), 0, DMAX).astype(jnp.int32)
    boat = set_ends(jax.random.randint(part_splits[5], (S,), 0, REC), jax.random.fold_in(part_splits[5], 1), 0, REC - 1).astype(jnp.int32)
    pair = draw_pair(jax.random.fold_in(jax.random.fold_in(arg_keys[7], part), 71), part)
    return dict(estimate=estimate, records=records, dip_receiver=dip_receiver, dip_source=dip_source, delays=delays, boat=boat, pair=pair)


step_size = 0.0625
filter_weight = 0.25
shrink_ratio = 0.3
HALF_ROOT = 0.7071067811865476

def place_trace(single, sample_lag, record_len):
    canvas = jnp.zeros((single.shape[0], record_len), single.dtype)
    return lax.dynamic_update_slice(canvas, single, (jnp.zeros((), jnp.int32), sample_lag.astype(jnp.int32)))

def cut_trace(row_data, sample_lag):
    return lax.dynamic_slice(row_data, (jnp.zeros((), jnp.int32), sample_lag.astype(jnp.int32)), (row_data.shape[0], NT))

def blend(current, delays, boat):
    shifted = jax.vmap(lambda single, sample_lag: place_trace(single, sample_lag, TB))(current, delays)
    onehot = (boat[None, :] == jnp.arange(REC, dtype=jnp.int32)[:, None]).astype(current.dtype)
    flattened = shifted.reshape(shifted.shape[0], -1)
    summed = jnp.dot(onehot, flattened, precision=lax.Precision.HIGHEST, preferred_element_type=jnp.float32)
    return summed.reshape(REC, current.shape[1], TB)

def unblend(residual, delays, boat):
    picked = jnp.take(residual, boat, axis=0)
    return jax.vmap(cut_trace)(picked, delays)

def predict(prior, dip_field):
    zero_column = jnp.zeros_like(prior[..., :1])
    earlier = jnp.concatenate([zero_column, prior[..., :-1]], axis=-1)
    later = jnp.concatenate([prior[..., 1:], zero_column], axis=-1)
    return earlier * dip_field * (dip_field + 1.0) * 0.5 + prior * (1.0 - dip_field * dip_field) + later * dip_field * (dip_field - 1.0) * 0.5

def soften(values, threshold):
    return values - jnp.clip(values, -threshold, threshold)

def shrink_haar(values, threshold):
    length = values.shape[-1]
    if length == 1:
        return soften(values, threshold)
    paired = values.reshape(values.shape[:-1] + (length // 2, 2))
    coarse = (paired[..., 0] + paired[..., 1]) * HALF_ROOT
    detail = (paired[..., 0] - paired[..., 1]) * HALF_ROOT
    coarse = shrink_haar(coarse, threshold)
    detail = soften(detail, threshold)
    joined = jnp.stack([(coarse + detail) * HALF_ROOT, (coarse - detail) * HALF_ROOT], axis=-1)
    return joined.reshape(values.shape)

def reference(estimate, records, dip_receiver, dip_source, delays, boat, pair):
    records_wide = records.astype(jnp.float32)
    receiver_dip = dip_receiver.astype(jnp.float32)
    source_dip = dip_source.astype(jnp.float32)
    current = estimate
    for iteration in range(ITERS):
        wide = current.astype(jnp.float32)
        predicted = blend(wide, delays, boat)
        residual = records_wide - predicted
        adjoint = unblend(residual, delays, boat)
        update = (wide + step_size * adjoint).astype(jnp.bfloat16)
        update_wide = update.astype(jnp.float32)
        energy = jnp.sum(update_wide * update_wide)
        threshold = shrink_ratio * jnp.sqrt(energy / (S * R * NT) + 1e-06)
        swapped = jnp.take(jnp.take(update, pair, axis=0), pair, axis=1).transpose(1, 0, 2)
        symmetric = (0.5 * (update_wide + swapped.astype(jnp.float32))).astype(jnp.bfloat16)
        sym_wide = symmetric.astype(jnp.float32)
        prior_receiver = jnp.concatenate([jnp.zeros_like(sym_wide[:, :1]), sym_wide[:, :-1]], axis=1)
        prior_source = jnp.concatenate([jnp.zeros_like(sym_wide[:1]), sym_wide[:-1]], axis=0)
        filtered = sym_wide - filter_weight * (sym_wide - predict(prior_receiver, receiver_dip) + (sym_wide - predict(prior_source, source_dip)))
        blocks = filtered.reshape(S, R, NT // WBLK, WBLK)
        current = shrink_haar(blocks, threshold).reshape(S, R, NT).astype(jnp.bfloat16)
    return current
```

```python
import functools
import math

import jax
import jax.numpy as jnp
import numpy as np
from jax import lax
from jax.experimental import pallas as pl
from jax.experimental.pallas import tpu as pltpu
from jax.sharding import PartitionSpec as P

WBLK = 256
ITERS = 2
LANES = 128

STEP_SIZE = 0.0625
SHRINK_RATIO = 0.3

F32 = jnp.float32
BF16 = jnp.bfloat16


def haar_signs(length):
    signs = np.zeros((length, length), np.float32)
    scales = np.zeros((1, length), np.float32)
    signs[0] = 1.0
    scales[0, 0] = 1.0 / math.sqrt(length)
    row, support = 1, length
    while support > 1:
        for start in range(0, length, support):
            signs[row, start : start + support // 2] = 1.0
            signs[row, start + support // 2 : start + support] = -1.0
            scales[0, row] = 1.0 / math.sqrt(support)
            row += 1
        support //= 2
    return signs, scales


def row_orders(n, local, blocks):
    total = n * local
    size = blocks * local * total
    slab = np.zeros((size, size), np.float32)
    node = np.zeros((size, size), np.float32)
    for d in range(n):
        for w in range(blocks):
            for sl in range(local):
                for j in range(local):
                    message = ((d * blocks + w) * local + sl) * local + j
                    slab[message, (w * local + sl) * total + d * local + j] = 1.0
                    node[(w * total + d * local + sl) * local + j, message] = 1.0
    return slab, node


def mm(a, b):
    return jnp.dot(a, b, preferred_element_type=F32)


def split_mm(a, b):
    high = a.astype(BF16)
    low = (a - high.astype(F32)).astype(BF16)
    return mm(high, b) + mm(low, b)


def turned(chunk, index):
    return jnp.take_along_axis(chunk, index, axis=1, mode="promise_in_bounds")


def kernel(
    n, local, samples, record_len, cells,
    est_ref, rec_ref, dipr_ref, dips_ref, delay_ref, onto_ref, back_ref, swap_ref,
    to_msg_ref, from_msg_ref, to_node_ref, from_node_ref, haar_t_ref, haar_ref, scale_ref,
    out_ref,
    cur, msg_a, got_a, msg_c, got_c, msg_e, got_e, msg_rim, got_rim,
    send_sem, recv_sem,
):
    me = lax.axis_index("src")
    total = n * local
    blocks = samples // WBLK
    chunks = samples // LANES
    per = blocks * local * local
    nodes = total * local

    barrier = pltpu.get_barrier_semaphore()

    @pl.loop(1, n)
    def _(k):
        pl.semaphore_signal(
            barrier, inc=1, device_id={"src": lax.rem(me + k, n)},
            device_id_type=pl.DeviceIdType.MESH,
        )

    def remote(src, dst, it, kind, target):
        return pltpu.make_async_remote_copy(
            src_ref=src, dst_ref=dst,
            send_sem=send_sem.at[it, kind], recv_sem=recv_sem.at[it, kind],
            device_id={"src": target}, device_id_type=pl.DeviceIdType.MESH,
        )

    def landed(buf, it, kind, sems):
        whole = buf.at[it, pl.ds(0, n - 1)]
        pltpu.make_async_copy(whole, whole, sems.at[it, kind]).wait()

    delay = delay_ref[...]
    lane = lax.broadcasted_iota(jnp.int32, delay.shape, 1)
    later_index = (lane - delay) & (LANES - 1)
    earlier_index = (lane + delay) & (LANES - 1)
    from_before = lane < delay
    from_same = lane < LANES - delay
    nothing = jnp.zeros(delay.shape, F32)

    for w in range(blocks):
        for sl in range(local):
            cur[pl.ds((w * local + sl) * total, total), :] = est_ref[sl, :, w * WBLK : (w + 1) * WBLK]

    scale = scale_ref[...]
    for it in range(ITERS):
        packed = mm(to_msg_ref[...], cur[...]).astype(BF16)
        msg_a[it] = packed.reshape(n, per, WBLK)
        got_a[it, me] = msg_a[it, me]
        if it == 0:
            pl.semaphore_wait(barrier, n - 1)

        @pl.loop(1, n)
        def _(k):
            target = lax.rem(me + k, n)
            remote(msg_a.at[it, target], got_a.at[it, me], it, 0, target).start()

        landed(got_a, it, 0, recv_sem)

        ordered = mm(to_node_ref[...], got_a[it].reshape(n * per, WBLK))
        wide = [
            ordered[(c // 2) * nodes : (c // 2 + 1) * nodes, (c % 2) * LANES : (c % 2 + 1) * LANES]
            for c in range(chunks)
        ]
        moved = [turned(chunk, later_index) for chunk in wide]
        placed = [
            jnp.where(
                from_before,
                moved[c - 1] if c > 0 else nothing,
                moved[c] if c < chunks else nothing,
            ).astype(BF16)
            for c in range(chunks + 1)
        ]
        predicted = mm(onto_ref[...], jnp.concatenate(placed, axis=1))
        residual = rec_ref[...] - predicted[: rec_ref.shape[0]]
        high = residual.astype(BF16).astype(F32)
        pieces = jnp.concatenate([high, residual - high], axis=0).astype(BF16)
        picked = mm(back_ref[...], pieces)
        moved = [
            turned(picked[:, c * LANES : (c + 1) * LANES], earlier_index) for c in range(chunks + 1)
        ]
        update = [
            (wide[c] + STEP_SIZE * jnp.where(from_same, moved[c], moved[c + 1])).astype(BF16)
            for c in range(chunks)
        ]
        square = nothing
        for piece in update:
            piece = piece.astype(F32)
            square = square + piece * piece
        msg_e[it] = jnp.sum(square, axis=0, keepdims=True)
        got_e[it, me] = msg_e[it]
        update_rows = jnp.concatenate(
            [jnp.concatenate(update[2 * w : 2 * w + 2], axis=1) for w in range(blocks)], axis=0
        )
        msg_c[it] = mm(from_node_ref[...], update_rows).astype(BF16).reshape(n, per, WBLK)
        got_c[it, me] = msg_c[it, me]

        @pl.loop(1, n)
        def _(k):
            target = lax.rem(me + k, n)
            remote(msg_c.at[it, target], got_c.at[it, me], it, 1, target).start()
            remote(msg_e.at[it], got_e.at[it, me], it, 2, target).start()

        swapped = mm(swap_ref[...], update_rows)
        landed(got_c, it, 1, recv_sem)
        symmetric = (
            0.5 * (mm(from_msg_ref[...], got_c[it].reshape(n * per, WBLK)) + swapped)
        ).astype(BF16)
        for w in range(blocks):
            start = (w * local + local - 1) * total
            msg_rim[it, w] = symmetric[start : start + total]

        @pl.when(me < n - 1)
        def _():
            remote(msg_rim.at[it], got_rim.at[it], it, 3, me + 1).start()

        @pl.when(me == 0)
        def _():
            got_rim[it] = jnp.zeros(got_rim.shape[1:], BF16)

        landed(got_e, it, 2, recv_sem)
        energy = jnp.sum(got_e[it].reshape(n, LANES))
        threshold = SHRINK_RATIO * jnp.sqrt(jnp.full((1, WBLK), energy) / cells + 1e-6)

        row = lax.broadcasted_iota(jnp.int32, (total, samples), 0)
        time = lax.broadcasted_iota(jnp.int32, (total, samples), 1)

        def terms(value):
            before = jnp.where(time == 0, 0.0, pltpu.roll(value, 1, axis=1))
            after = jnp.where(time == samples - 1, 0.0, pltpu.roll(value, samples - 1, axis=1))
            return value, 0.5 * (before - after), 0.5 * (before + after) - value

        def below(value):
            return jnp.where(row == 0, 0.0, pltpu.roll(value, 1, axis=0))

        def along(parts, dip):
            value, slope, bend = parts
            return value + dip * (slope + dip * bend)

        own = [
            terms(
                jnp.concatenate(
                    [
                        symmetric[(w * local + sl) * total : (w * local + sl + 1) * total]
                        for w in range(blocks)
                    ],
                    axis=1,
                ).astype(F32)
            )
            for sl in range(local)
        ]

        for sl in reversed(range(local)):
            if sl == 0:
                @pl.when(me > 0)
                def _():
                    remote(msg_rim.at[it], got_rim.at[it], it, 3, me).wait_recv()

                prior = terms(
                    jnp.concatenate([got_rim[it, w] for w in range(blocks)], axis=1).astype(F32)
                )
            else:
                prior = own[sl - 1]
            filtered = 0.5 * own[sl][0] + 0.25 * (
                along([below(part) for part in own[sl]], dipr_ref[sl].astype(F32))
                + along(prior, dips_ref[sl].astype(F32))
            )
            rows = jnp.concatenate(
                [filtered[:, w * WBLK : (w + 1) * WBLK] for w in range(blocks)], axis=0
            )
            coeffs = split_mm(rows, haar_t_ref[...]) * scale
            shrunk = coeffs - jnp.clip(coeffs, -threshold, threshold)
            restored = split_mm(shrunk * scale, haar_ref[...]).astype(BF16)
            for w in range(blocks):
                piece = restored[w * total : (w + 1) * total]
                if it == ITERS - 1:
                    out_ref[sl, :, w * WBLK : (w + 1) * WBLK] = piece
                else:
                    cur[pl.ds((w * local + sl) * total, total), :] = piece

    for it in range(ITERS):
        landed(msg_a, it, 0, send_sem)
        landed(msg_c, it, 1, send_sem)
        landed(got_e, it, 2, send_sem)

        @pl.when(me < n - 1)
        def _():
            remote(msg_rim.at[it], got_rim.at[it], it, 3, me + 1).wait_send()


def body(n, estimate, records, dip_receiver, dip_source, delays, boat, pair):
    local, receivers, samples = estimate.shape
    total = delays.shape[0]
    record_count, local_recv, record_len = records.shape
    blocks = samples // WBLK
    cells = total * receivers * samples
    nodes = total * local
    kinds = record_count * local
    signs, scales = haar_signs(WBLK)
    slab, node = row_orders(n, local, blocks)
    me = lax.axis_index("src")

    record_rows = records.reshape(kinds, record_len).astype(F32)
    delay_rows = jnp.broadcast_to(jnp.repeat(delays, local)[:, None], (nodes, LANES))
    boat_rows = jnp.repeat(boat, local) * local + jnp.arange(nodes, dtype=jnp.int32) % local
    padded = max(16, kinds)
    onto = (jnp.arange(padded, dtype=jnp.int32)[:, None] == boat_rows[None, :]).astype(BF16)
    back = (
        boat_rows[:, None] == (jnp.arange(2 * kinds, dtype=jnp.int32) % kinds)[None, :]
    ).astype(BF16)
    local_pair = lax.dynamic_slice_in_dim(pair, me * local, local) - me * local
    place = (
        jnp.arange(blocks, dtype=jnp.int32)[:, None, None] * nodes
        + local_pair[None, :, None]
        + pair[None, None, :] * local
    ).reshape(-1)
    size = blocks * nodes
    swap = (place[:, None] == jnp.arange(size, dtype=jnp.int32)[None, :]).astype(BF16)

    per = blocks * local * local
    vmem = pl.BlockSpec(memory_space=pltpu.VMEM)
    return pl.pallas_call(
        functools.partial(kernel, n, local, samples, record_len, float(cells)),
        out_shape=jax.ShapeDtypeStruct(estimate.shape, BF16),
        in_specs=[vmem] * 15,
        out_specs=vmem,
        scratch_shapes=[
            pltpu.VMEM((size, WBLK), BF16),
            pltpu.VMEM((ITERS, n, per, WBLK), BF16),
            pltpu.VMEM((ITERS, n, per, WBLK), BF16),
            pltpu.VMEM((ITERS, n, per, WBLK), BF16),
            pltpu.VMEM((ITERS, n, per, WBLK), BF16),
            pltpu.VMEM((ITERS, 1, LANES), F32),
            pltpu.VMEM((ITERS, n, 1, LANES), F32),
            pltpu.VMEM((ITERS, blocks, total, WBLK), BF16),
            pltpu.VMEM((ITERS, blocks, total, WBLK), BF16),
            pltpu.SemaphoreType.DMA((ITERS, 4)),
            pltpu.SemaphoreType.DMA((ITERS, 4)),
        ],
        compiler_params=pltpu.CompilerParams(
            collective_id=0, has_side_effects=True, vmem_limit_bytes=48 * 1024 * 1024
        ),
    )(
        estimate, record_rows, dip_receiver, dip_source, delay_rows, onto, back, swap,
        jnp.asarray(slab, BF16), jnp.asarray(slab.T, BF16),
        jnp.asarray(node, BF16), jnp.asarray(node.T, BF16),
        jnp.asarray(signs.T, BF16), jnp.asarray(signs, BF16), jnp.asarray(scales, F32),
    )


def solution(mesh):
    return jax.shard_map(
        functools.partial(body, mesh.shape["src"]),
        mesh=mesh,
        in_specs=(
            P(("parts", "src"), None, None),
            P("parts", "src", None),
            P(("parts", "src"), None, None),
            P(("parts", "src"), None, None),
            P("parts"),
            P("parts"),
            P("parts"),
        ),
        out_specs=P(("parts", "src"), None, None),
        check_vma=False,
    )
```

```python
import functools
import math

import jax
import jax.numpy as jnp
import numpy as np
from jax import lax
from jax.experimental import pallas as pl
from jax.experimental.pallas import tpu as pltpu
from jax.sharding import PartitionSpec as P

WBLK = 256
ITERS = 2
LANES = 128

STEP_SIZE = 0.0625
SHRINK_RATIO = 0.3

F32 = jnp.float32
BF16 = jnp.bfloat16


def haar_signs(length):
    signs = np.zeros((length, length), np.float32)
    scales = np.zeros((1, length), np.float32)
    signs[0] = 1.0
    scales[0, 0] = 1.0 / math.sqrt(length)
    row, support = 1, length
    while support > 1:
        for start in range(0, length, support):
            signs[row, start : start + support // 2] = 1.0
            signs[row, start + support // 2 : start + support] = -1.0
            scales[0, row] = 1.0 / math.sqrt(support)
            row += 1
        support //= 2
    return signs, scales


def row_orders(n, local, blocks):
    total = n * local
    size = blocks * local * total
    slab = np.zeros((size, size), np.float32)
    node = np.zeros((size, size), np.float32)
    for d in range(n):
        for w in range(blocks):
            for sl in range(local):
                for j in range(local):
                    message = ((d * blocks + w) * local + sl) * local + j
                    slab[message, (w * local + sl) * total + d * local + j] = 1.0
                    node[(w * total + d * local + sl) * local + j, message] = 1.0
    return slab, node


def mm(a, b):
    return jnp.dot(a, b, preferred_element_type=F32)


def split_mm(a, b):
    high = a.astype(BF16)
    low = (a - high.astype(F32)).astype(BF16)
    return mm(high, b) + mm(low, b)


def turned(chunk, index):
    return jnp.take_along_axis(chunk, index, axis=1, mode="promise_in_bounds")


def by_row(values, rows, per_row):
    shape = (rows, values.shape[1])
    wanted = lax.broadcasted_iota(jnp.int32, shape, 0) // per_row
    lane = lax.broadcasted_iota(jnp.int32, shape, 1)
    return jnp.sum(jnp.where(lane == wanted, values, 0), axis=1, keepdims=True)


def prepare(
    local, total, blocks, me, rec_in, delays_ref, boat_ref, pair_ref,
    rec_ref, delay_ref, onto_ref, back_ref, swap_ref,
):
    nodes = total * local
    kinds = rec_in.shape[0] * local
    for b in range(rec_in.shape[0]):
        rec_ref[b * local : (b + 1) * local, :] = rec_in[b].astype(F32)
    delay_ref[...] = jnp.broadcast_to(by_row(delays_ref[...], nodes, local), delay_ref.shape)
    own = lax.broadcasted_iota(jnp.int32, (nodes, 1), 0) % local
    kind = by_row(boat_ref[...], nodes, local) * local + own
    column = lax.broadcasted_iota(jnp.int32, back_ref.shape, 1) % kinds
    back_ref[...] = jnp.where(kind == column, 1.0, 0.0).astype(BF16)
    column = lax.broadcasted_iota(jnp.int32, (nodes, onto_ref.shape[0]), 1)
    onto_ref[...] = jnp.where(kind == column, 1.0, 0.0).T.astype(BF16)
    pairs = pair_ref[...]
    partner = by_row(pairs, total, 1) * local
    lane = lax.broadcasted_iota(jnp.int32, pairs.shape, 1)
    column = lax.broadcasted_iota(jnp.int32, (total, swap_ref.shape[1]), 1)
    for sl in range(local):
        first = me * local
        mate = jnp.sum(jnp.where(lane == first + sl, pairs - first, 0), axis=1, keepdims=True)
        for w in range(blocks):
            start = (w * local + sl) * total
            swap_ref[start : start + total, :] = jnp.where(
                column == partner + (mate + w * nodes), 1.0, 0.0
            ).astype(BF16)


def kernel(
    n, local, samples, record_len, cells,
    est_hbm, rec_hbm, dipr_hbm, dips_hbm, delays_hbm, boat_hbm, pair_hbm,
    to_msg_hbm, from_msg_hbm, to_node_hbm, from_node_hbm, haar_t_hbm, haar_hbm, scale_ref,
    out_ref,
    cur, msg_a, got_a, msg_c, got_c, msg_e, got_e, msg_rim, got_rim,
    est_ref, rec_in, dipr_ref, dips_ref, delays_ref, boat_ref, pair_ref,
    to_msg_ref, from_msg_ref, to_node_ref, from_node_ref, haar_t_ref, haar_ref,
    rec_ref, delay_ref, onto_ref, back_ref, swap_ref,
    send_sem, recv_sem, load_sem,
):
    me = lax.axis_index("src")
    total = n * local
    blocks = samples // WBLK
    chunks = samples // LANES
    per = blocks * local * local
    nodes = total * local

    loads = [
        pltpu.make_async_copy(src, dst, load_sem.at[i])
        for i, (src, dst) in enumerate(
            [
                (est_hbm, est_ref), (to_msg_hbm, to_msg_ref), (delays_hbm, delays_ref),
                (boat_hbm, boat_ref), (pair_hbm, pair_ref), (rec_hbm, rec_in),
                (to_node_hbm, to_node_ref), (from_node_hbm, from_node_ref),
                (from_msg_hbm, from_msg_ref), (dipr_hbm, dipr_ref), (dips_hbm, dips_ref),
                (haar_t_hbm, haar_t_ref), (haar_hbm, haar_ref),
            ]
        )
    ]
    for load in loads:
        load.start()

    barrier = pltpu.get_barrier_semaphore()

    @pl.loop(1, n)
    def _(k):
        pl.semaphore_signal(
            barrier, inc=1, device_id={"src": lax.rem(me + k, n)},
            device_id_type=pl.DeviceIdType.MESH,
        )

    def remote(src, dst, it, kind, target):
        return pltpu.make_async_remote_copy(
            src_ref=src, dst_ref=dst,
            send_sem=send_sem.at[it, kind], recv_sem=recv_sem.at[it, kind],
            device_id={"src": target}, device_id_type=pl.DeviceIdType.MESH,
        )

    def landed(buf, it, kind, sems):
        whole = buf.at[it, pl.ds(0, n - 1)]
        pltpu.make_async_copy(whole, whole, sems.at[it, kind]).wait()

    loads[0].wait()
    loads[1].wait()
    for w in range(blocks):
        for sl in range(local):
            cur[pl.ds((w * local + sl) * total, total), :] = est_ref[sl, :, w * WBLK : (w + 1) * WBLK]

    scale = scale_ref[...]
    for it in range(ITERS):
        packed = mm(to_msg_ref[...], cur[...]).astype(BF16)
        msg_a[it] = packed.reshape(n, per, WBLK)
        got_a[it, me] = msg_a[it, me]
        if it == 0:
            pl.semaphore_wait(barrier, n - 1)

        @pl.loop(1, n)
        def _(k):
            target = lax.rem(me + k, n)
            remote(msg_a.at[it, target], got_a.at[it, me], it, 0, target).start()

        if it == 0:
            for load in loads[2:]:
                load.wait()
            prepare(
                local, total, blocks, me, rec_in, delays_ref, boat_ref, pair_ref,
                rec_ref, delay_ref, onto_ref, back_ref, swap_ref,
            )

        delay = delay_ref[...]
        lane = lax.broadcasted_iota(jnp.int32, delay.shape, 1)
        later_index = (lane - delay) & (LANES - 1)
        earlier_index = (lane + delay) & (LANES - 1)
        from_before = lane < delay
        from_same = lane < LANES - delay
        nothing = jnp.zeros(delay.shape, F32)
        landed(got_a, it, 0, recv_sem)

        ordered = mm(to_node_ref[...], got_a[it].reshape(n * per, WBLK))
        wide = [
            ordered[(c // 2) * nodes : (c // 2 + 1) * nodes, (c % 2) * LANES : (c % 2 + 1) * LANES]
            for c in range(chunks)
        ]
        moved = [turned(chunk, later_index) for chunk in wide]
        placed = [
            jnp.where(
                from_before,
                moved[c - 1] if c > 0 else nothing,
                moved[c] if c < chunks else nothing,
            ).astype(BF16)
            for c in range(chunks + 1)
        ]
        predicted = mm(onto_ref[...], jnp.concatenate(placed, axis=1))
        residual = rec_ref[...] - predicted[: rec_ref.shape[0]]
        high = residual.astype(BF16).astype(F32)
        pieces = jnp.concatenate([high, residual - high], axis=0).astype(BF16)
        picked = mm(back_ref[...], pieces)
        moved = [
            turned(picked[:, c * LANES : (c + 1) * LANES], earlier_index) for c in range(chunks + 1)
        ]
        update = [
            (wide[c] + STEP_SIZE * jnp.where(from_same, moved[c], moved[c + 1])).astype(BF16)
            for c in range(chunks)
        ]
        square = nothing
        for piece in update:
            piece = piece.astype(F32)
            square = square + piece * piece
        msg_e[it] = jnp.sum(square, axis=0, keepdims=True)
        got_e[it, me] = msg_e[it]
        update_rows = jnp.concatenate(
            [jnp.concatenate(update[2 * w : 2 * w + 2], axis=1) for w in range(blocks)], axis=0
        )
        msg_c[it] = mm(from_node_ref[...], update_rows).astype(BF16).reshape(n, per, WBLK)
        got_c[it, me] = msg_c[it, me]

        @pl.loop(1, n)
        def _(k):
            target = lax.rem(me + k, n)
            remote(msg_c.at[it, target], got_c.at[it, me], it, 1, target).start()
            remote(msg_e.at[it], got_e.at[it, me], it, 2, target).start()

        swapped = mm(swap_ref[...], update_rows)
        landed(got_c, it, 1, recv_sem)
        symmetric = (
            0.5 * (mm(from_msg_ref[...], got_c[it].reshape(n * per, WBLK)) + swapped)
        ).astype(BF16)
        for w in range(blocks):
            start = (w * local + local - 1) * total
            msg_rim[it, w] = symmetric[start : start + total]

        @pl.when(me < n - 1)
        def _():
            remote(msg_rim.at[it], got_rim.at[it], it, 3, me + 1).start()

        @pl.when(me == 0)
        def _():
            got_rim[it] = jnp.zeros(got_rim.shape[1:], BF16)

        landed(got_e, it, 2, recv_sem)
        energy = jnp.sum(got_e[it].reshape(n, LANES))
        threshold = SHRINK_RATIO * jnp.sqrt(jnp.full((1, WBLK), energy) / cells + 1e-6)

        row = lax.broadcasted_iota(jnp.int32, (total, samples), 0)
        time = lax.broadcasted_iota(jnp.int32, (total, samples), 1)

        def terms(value):
            before = jnp.where(time == 0, 0.0, pltpu.roll(value, 1, axis=1))
            after = jnp.where(time == samples - 1, 0.0, pltpu.roll(value, samples - 1, axis=1))
            return value, 0.5 * (before - after), 0.5 * (before + after) - value

        def below(value):
            return jnp.where(row == 0, 0.0, pltpu.roll(value, 1, axis=0))

        def along(parts, dip):
            value, slope, bend = parts
            return value + dip * (slope + dip * bend)

        own = [
            terms(
                jnp.concatenate(
                    [
                        symmetric[(w * local + sl) * total : (w * local + sl + 1) * total]
                        for w in range(blocks)
                    ],
                    axis=1,
                ).astype(F32)
            )
            for sl in range(local)
        ]

        for sl in reversed(range(local)):
            if sl == 0:
                @pl.when(me > 0)
                def _():
                    remote(msg_rim.at[it], got_rim.at[it], it, 3, me).wait_recv()

                prior = terms(
                    jnp.concatenate([got_rim[it, w] for w in range(blocks)], axis=1).astype(F32)
                )
            else:
                prior = own[sl - 1]
            filtered = 0.5 * own[sl][0] + 0.25 * (
                along([below(part) for part in own[sl]], dipr_ref[sl].astype(F32))
                + along(prior, dips_ref[sl].astype(F32))
            )
            rows = jnp.concatenate(
                [filtered[:, w * WBLK : (w + 1) * WBLK] for w in range(blocks)], axis=0
            )
            coeffs = split_mm(rows, haar_t_ref[...]) * scale
            shrunk = coeffs - jnp.clip(coeffs, -threshold, threshold)
            restored = split_mm(shrunk * scale, haar_ref[...]).astype(BF16)
            for w in range(blocks):
                piece = restored[w * total : (w + 1) * total]
                if it == ITERS - 1:
                    out_ref[sl, :, w * WBLK : (w + 1) * WBLK] = piece
                else:
                    cur[pl.ds((w * local + sl) * total, total), :] = piece

    for it in range(ITERS):
        landed(msg_a, it, 0, send_sem)
        landed(msg_c, it, 1, send_sem)
        landed(got_e, it, 2, send_sem)

        @pl.when(me < n - 1)
        def _():
            remote(msg_rim.at[it], got_rim.at[it], it, 3, me + 1).wait_send()


def body(n, estimate, records, dip_receiver, dip_source, delays, boat, pair):
    local, receivers, samples = estimate.shape
    total = delays.shape[0]
    record_count, local_recv, record_len = records.shape
    blocks = samples // WBLK
    cells = total * receivers * samples
    nodes = total * local
    kinds = record_count * local
    signs, scales = haar_signs(WBLK)
    slab, node = row_orders(n, local, blocks)
    padded = max(16, kinds)
    size = blocks * nodes

    per = blocks * local * local
    vmem = pl.BlockSpec(memory_space=pltpu.VMEM)
    return pl.pallas_call(
        functools.partial(kernel, n, local, samples, record_len, float(cells)),
        out_shape=jax.ShapeDtypeStruct(estimate.shape, BF16),
        in_specs=[pl.BlockSpec(memory_space=pl.ANY)] * 13 + [vmem],
        out_specs=vmem,
        scratch_shapes=[
            pltpu.VMEM((size, WBLK), BF16),
            pltpu.VMEM((ITERS, n, per, WBLK), BF16),
            pltpu.VMEM((ITERS, n, per, WBLK), BF16),
            pltpu.VMEM((ITERS, n, per, WBLK), BF16),
            pltpu.VMEM((ITERS, n, per, WBLK), BF16),
            pltpu.VMEM((ITERS, 1, LANES), F32),
            pltpu.VMEM((ITERS, n, 1, LANES), F32),
            pltpu.VMEM((ITERS, blocks, total, WBLK), BF16),
            pltpu.VMEM((ITERS, blocks, total, WBLK), BF16),
            pltpu.VMEM(estimate.shape, BF16),
            pltpu.VMEM(records.shape, BF16),
            pltpu.VMEM(estimate.shape, BF16),
            pltpu.VMEM(estimate.shape, BF16),
            pltpu.VMEM((1, total), jnp.int32),
            pltpu.VMEM((1, total), jnp.int32),
            pltpu.VMEM((1, total), jnp.int32),
            pltpu.VMEM((size, size), BF16),
            pltpu.VMEM((size, size), BF16),
            pltpu.VMEM((size, size), BF16),
            pltpu.VMEM((size, size), BF16),
            pltpu.VMEM((WBLK, WBLK), BF16),
            pltpu.VMEM((WBLK, WBLK), BF16),
            pltpu.VMEM((kinds, record_len), F32),
            pltpu.VMEM((nodes, LANES), jnp.int32),
            pltpu.VMEM((padded, nodes), BF16),
            pltpu.VMEM((nodes, 2 * kinds), BF16),
            pltpu.VMEM((size, size), BF16),
            pltpu.SemaphoreType.DMA((ITERS, 4)),
            pltpu.SemaphoreType.DMA((ITERS, 4)),
            pltpu.SemaphoreType.DMA((13,)),
        ],
        compiler_params=pltpu.CompilerParams(
            collective_id=0, has_side_effects=True, vmem_limit_bytes=60 * 1024 * 1024
        ),
    )(
        estimate, records, dip_receiver, dip_source,
        delays.reshape(1, total), boat.reshape(1, total), pair.reshape(1, total),
        jnp.asarray(slab, BF16), jnp.asarray(slab.T, BF16),
        jnp.asarray(node, BF16), jnp.asarray(node.T, BF16),
        jnp.asarray(signs.T, BF16), jnp.asarray(signs, BF16), jnp.asarray(scales, F32),
    )


def solution(mesh):
    return jax.shard_map(
        functools.partial(body, mesh.shape["src"]),
        mesh=mesh,
        in_specs=(
            P(("parts", "src"), None, None),
            P("parts", "src", None),
            P(("parts", "src"), None, None),
            P(("parts", "src"), None, None),
            P("parts"),
            P("parts"),
            P("parts"),
        ),
        out_specs=P(("parts", "src"), None, None),
        check_vma=False,
    )
```

```python
import functools
import math

import jax
import jax.numpy as jnp
from jax import lax
from jax.experimental import pallas as pl
from jax.experimental.pallas import tpu as pltpu
from jax.sharding import PartitionSpec as P

WBLK = 256
ITERS = 2
LANES = 128

STEP_SIZE = 0.0625
SHRINK_RATIO = 0.3

F32 = jnp.float32
BF16 = jnp.bfloat16


def one_hot(ref, column_of):
    wanted = column_of(lax.broadcasted_iota(jnp.int32, (ref.shape[0], 1), 0))
    column = lax.broadcasted_iota(jnp.int32, ref.shape, 1)
    ref[...] = jnp.where(column == wanted, 1.0, 0.0).astype(BF16)


def order_maps(n, local, blocks):
    total = n * local

    def slab_of_message(i):
        j, sl = i % local, i // local % local
        w, d = i // (local * local) % blocks, i // (local * local * blocks)
        return ((w * local + sl) * n + d) * local + j

    def message_of_slab(i):
        j, d = i % local, i // local % n
        sl, w = i // total % local, i // (total * local)
        return ((d * blocks + w) * local + sl) * local + j

    def message_of_node(i):
        sl, d = i % local, i // local % n
        j, w = i // total % local, i // (total * local)
        return ((d * blocks + w) * local + sl) * local + j

    def node_of_message(i):
        j, sl = i % local, i // local % local
        w, d = i // (local * local) % blocks, i // (local * local * blocks)
        return ((w * local + j) * n + d) * local + sl

    return slab_of_message, message_of_slab, message_of_node, node_of_message


def haar_supports(index):
    support = jnp.full(index.shape, WBLK, jnp.int32)
    first = jnp.ones(index.shape, jnp.int32)
    level = 2
    while level < WBLK:
        support = jnp.where(index >= level, WBLK // level, support)
        first = jnp.where(index >= level, level, first)
        level *= 2
    start = jnp.where(index == 0, 0, (index - first) * support)
    middle = jnp.where(index == 0, WBLK, start + support // 2)
    return start, middle, start + support


def haar_signs(ref, coefficient_axis):
    shape = (WBLK, 1) if coefficient_axis == 0 else (1, WBLK)
    start, middle, end = haar_supports(lax.broadcasted_iota(jnp.int32, shape, coefficient_axis))
    time = lax.broadcasted_iota(jnp.int32, (WBLK, WBLK), 1 - coefficient_axis)
    inside = jnp.where((time >= start) & (time < middle), 1.0, 0.0)
    ref[...] = (inside - jnp.where((time >= middle) & (time < end), 1.0, 0.0)).astype(BF16)


def haar_scales():
    index = lax.broadcasted_iota(jnp.int32, (1, WBLK), 1)
    scale = jnp.full(index.shape, 1.0 / math.sqrt(WBLK), F32)
    level = 2
    while level < WBLK:
        scale = jnp.where(index >= level, math.sqrt(level / WBLK), scale)
        level *= 2
    return scale


def mm(a, b):
    return jnp.dot(a, b, preferred_element_type=F32)


def split_mm(a, b):
    high = a.astype(BF16)
    low = (a - high.astype(F32)).astype(BF16)
    return mm(high, b) + mm(low, b)


def turned(chunk, index):
    return jnp.take_along_axis(chunk, index, axis=1, mode="promise_in_bounds")


def by_row(values, rows):
    shape = (rows, values.shape[1])
    wanted = lax.broadcasted_iota(jnp.int32, shape, 0) % values.shape[1]
    lane = lax.broadcasted_iota(jnp.int32, shape, 1)
    return jnp.sum(jnp.where(lane == wanted, values, 0), axis=1, keepdims=True)


def prepare(
    local, total, blocks, me, rec_in, delays_ref, boat_ref, pair_ref,
    rec_ref, delay_ref, onto_ref, back_ref, swap_ref, swap_msg_ref,
):
    nodes = total * local
    kinds = rec_in.shape[0] * local
    for b in range(rec_in.shape[0]):
        rec_ref[b * local : (b + 1) * local, :] = rec_in[b].astype(F32)
    delay_ref[...] = jnp.broadcast_to(by_row(delays_ref[...], nodes), delay_ref.shape)
    own = lax.broadcasted_iota(jnp.int32, (nodes, 1), 0) // total
    kind = by_row(boat_ref[...], nodes) * local + own
    column = lax.broadcasted_iota(jnp.int32, back_ref.shape, 1) % kinds
    back_ref[...] = jnp.where(kind == column, 1.0, 0.0).astype(BF16)
    column = lax.broadcasted_iota(jnp.int32, (nodes, onto_ref.shape[0]), 1)
    onto_ref[...] = jnp.where(kind == column, 1.0, 0.0).T.astype(BF16)
    pairs = pair_ref[...]
    partner = by_row(pairs, total)
    partner_msg = partner // local * (blocks * local * local) + partner % local
    lane = lax.broadcasted_iota(jnp.int32, pairs.shape, 1)
    column = lax.broadcasted_iota(jnp.int32, (total, swap_ref.shape[1]), 1)
    for sl in range(local):
        first = me * local
        mate = jnp.sum(jnp.where(lane == first + sl, pairs - first, 0), axis=1, keepdims=True)
        for w in range(blocks):
            start = (w * local + sl) * total
            swap_ref[start : start + total, :] = jnp.where(
                column == partner + (mate + w * local) * total, 1.0, 0.0
            ).astype(BF16)
            swap_msg_ref[start : start + total, :] = jnp.where(
                column == partner_msg + (mate + w * local) * local, 1.0, 0.0
            ).astype(BF16)


def by_slab(rows, at, local, total):
    count = rows.shape[0] // (local * total)
    return jnp.concatenate(
        [rows[(w * local + at) * total : (w * local + at + 1) * total] for w in range(count)],
        axis=1,
    )


def terms(value):
    samples = value.shape[1]
    time = lax.broadcasted_iota(jnp.int32, value.shape, 1)
    before = jnp.where(time == 0, 0.0, pltpu.roll(value, 1, axis=1))
    after = jnp.where(time == samples - 1, 0.0, pltpu.roll(value, samples - 1, axis=1))
    return value, 0.5 * (before - after), 0.5 * (before + after) - value


def below(value):
    row = lax.broadcasted_iota(jnp.int32, value.shape, 0)
    return jnp.where(row == 0, 0.0, pltpu.roll(value, 1, axis=0))


def along(parts, dip):
    value, slope, bend = parts
    return value + dip * (slope + dip * bend)


def kernel(
    n, local, samples, cells,
    est_hbm, rec_hbm, dipr_hbm, dips_hbm, delays_hbm, boat_hbm, pair_hbm,
    out_ref,
    cur, msg_a, got_a, msg_d, got_d, msg_c, got_c, msg_e, got_e, msg_rim, got_rim,
    est_ref, rec_in, dipr_ref, dips_ref, delays_ref, boat_ref, pair_ref,
    to_msg_ref, from_msg_ref, to_node_ref, from_node_ref, haar_t_ref, haar_ref,
    rec_ref, delay_ref, onto_ref, back_ref, swap_ref, swap_msg_ref, dip_node,
    send_sem, recv_sem, load_sem,
):
    me = lax.axis_index("src")
    total = n * local
    blocks = samples // WBLK
    chunks = samples // LANES
    per = blocks * local * local
    nodes = total * local

    barrier = pltpu.get_barrier_semaphore()

    @pl.loop(1, n)
    def _(k):
        pl.semaphore_signal(
            barrier, inc=1, device_id={"src": lax.rem(me + k, n)},
            device_id_type=pl.DeviceIdType.MESH,
        )

    loads = [
        pltpu.make_async_copy(src, dst, load_sem.at[i])
        for i, (src, dst) in enumerate(
            [
                (est_hbm, est_ref), (dipr_hbm, dipr_ref), (dips_hbm, dips_ref),
                (delays_hbm, delays_ref), (boat_hbm, boat_ref), (pair_hbm, pair_ref),
                (rec_hbm, rec_in),
            ]
        )
    ]
    for load in loads:
        load.start()

    def remote(src, dst, it, kind, target):
        return pltpu.make_async_remote_copy(
            src_ref=src, dst_ref=dst,
            send_sem=send_sem.at[it, kind], recv_sem=recv_sem.at[it, kind],
            device_id={"src": target}, device_id_type=pl.DeviceIdType.MESH,
        )

    def landed(buf, it, kind, sems):
        whole = buf.at[pl.ds(0, n - 1)]
        pltpu.make_async_copy(whole, whole, sems.at[it, kind]).wait()

    slab_of_message, message_of_slab, message_of_node, node_of_message = order_maps(
        n, local, blocks
    )
    one_hot(to_msg_ref, slab_of_message)

    def packed(ref):
        rows = jnp.concatenate(
            [
                ref[sl, :, w * WBLK : (w + 1) * WBLK]
                for w in range(blocks)
                for sl in range(local)
            ],
            axis=0,
        )
        return mm(to_msg_ref[...], rows).astype(BF16).reshape(n, per, WBLK)

    loads[0].wait()
    msg_a[...] = packed(est_ref)
    got_a[me] = msg_a[me]
    loads[1].wait()
    loads[2].wait()
    msg_d[:, :per, :] = packed(dipr_ref)
    msg_d[:, per:, :] = packed(dips_ref)
    got_d[me] = msg_d[me]
    pl.semaphore_wait(barrier, n - 1)

    @pl.loop(1, n)
    def _(k):
        target = lax.rem(me + n - k, n)
        remote(msg_a.at[target], got_a.at[me], 0, 0, target).start()

    @pl.loop(1, n)
    def _(k):
        target = lax.rem(me + n - k, n)
        remote(msg_d.at[target], got_d.at[me], 0, 4, target).start()

    for load in loads[3:]:
        load.wait()
    one_hot(to_node_ref, message_of_node)
    prepare(
        local, total, blocks, me, rec_in, delays_ref, boat_ref, pair_ref,
        rec_ref, delay_ref, onto_ref, back_ref, swap_ref, swap_msg_ref,
    )
    one_hot(from_node_ref, node_of_message)
    one_hot(from_msg_ref, message_of_slab)
    haar_signs(haar_t_ref, 1)
    haar_signs(haar_ref, 0)
    scale = haar_scales()

    landed(got_a, 0, 0, recv_sem)
    cur[...] = mm(to_node_ref[...], got_a[...].reshape(n * per, WBLK))

    for it in range(ITERS):
        last = it == ITERS - 1
        delay = delay_ref[...]
        lane = lax.broadcasted_iota(jnp.int32, delay.shape, 1)
        later_index = (lane - delay) & (LANES - 1)
        earlier_index = (lane + delay) & (LANES - 1)
        from_before = lane < delay
        from_same = lane < LANES - delay
        nothing = jnp.zeros(delay.shape, F32)
        wide = [
            cur[(c // 2) * nodes : (c // 2 + 1) * nodes, (c % 2) * LANES : (c % 2 + 1) * LANES]
            for c in range(chunks)
        ]
        moved = [turned(chunk, later_index) for chunk in wide]
        placed = [
            jnp.where(
                from_before,
                moved[c - 1] if c > 0 else nothing,
                moved[c] if c < chunks else nothing,
            ).astype(BF16)
            for c in range(chunks + 1)
        ]
        predicted = mm(onto_ref[...], jnp.concatenate(placed, axis=1))
        residual = rec_ref[...] - predicted[: rec_ref.shape[0]]
        high = residual.astype(BF16).astype(F32)
        pieces = jnp.concatenate([high, residual - high], axis=0).astype(BF16)
        picked = mm(back_ref[...], pieces)
        moved = [
            turned(picked[:, c * LANES : (c + 1) * LANES], earlier_index) for c in range(chunks + 1)
        ]
        update = [
            (wide[c] + STEP_SIZE * jnp.where(from_same, moved[c], moved[c + 1])).astype(BF16)
            for c in range(chunks)
        ]
        update_rows = jnp.concatenate(
            [jnp.concatenate(update[2 * w : 2 * w + 2], axis=1) for w in range(blocks)], axis=0
        )
        msg_c[it] = mm(from_node_ref[...], update_rows).astype(BF16).reshape(n, per, WBLK)

        @pl.loop(1, n)
        def _(k):
            target = lax.rem(me + n - k, n)
            remote(msg_c.at[it, target], got_c.at[it, me], it, 1, target).start()

        square = nothing
        for piece in update:
            piece = piece.astype(F32)
            square = square + piece * piece
        msg_e[it] = jnp.sum(square, axis=0, keepdims=True)

        @pl.loop(1, n)
        def _(k):
            target = lax.rem(me + n - k, n)
            remote(msg_e.at[it], got_e.at[it, me], it, 2, target).start()

        got_e[it, me] = msg_e[it]
        got_c[it, me] = msg_c[it, me]

        if not last:
            landed(got_d, 0, 4, recv_sem)
            for i in range(2):
                rows = got_d[:, i * per : (i + 1) * per, :].reshape(n * per, WBLK)
                dip_node[i] = mm(to_node_ref[...], rows).astype(BF16)
            kept = update_rows.astype(F32)
        else:
            kept = mm(swap_ref[...], update_rows)
        arrange = from_msg_ref if last else swap_msg_ref
        landed(got_c.at[it], it, 1, recv_sem)
        symmetric = (
            0.5 * (mm(arrange[...], got_c[it].reshape(n * per, WBLK)) + kept)
        ).astype(BF16)
        for w in range(blocks):
            start = (w * local + local - 1) * total
            msg_rim[it, w] = symmetric[start : start + total]

        @pl.when(me < n - 1)
        def _():
            remote(msg_rim.at[it], got_rim.at[it], it, 3, me + 1).start()

        @pl.when(me == 0)
        def _():
            got_rim[it] = jnp.zeros(got_rim.shape[1:], BF16)

        own = [terms(by_slab(symmetric, at, local, total).astype(F32)) for at in range(local)]

        landed(got_e.at[it], it, 2, recv_sem)
        energy = jnp.sum(got_e[it].reshape(n, LANES))
        threshold = SHRINK_RATIO * jnp.sqrt(jnp.full((1, WBLK), energy) / cells + 1e-6)

        for at in reversed(range(local)):
            if last:
                within, across = dipr_ref[at], dips_ref[at]
            else:
                within = by_slab(dip_node[1], at, local, total)
                across = by_slab(dip_node[0], at, local, total)
            inside = along([below(part) for part in own[at]], within.astype(F32))
            if at == 0:
                @pl.when(me > 0)
                def _():
                    remote(msg_rim.at[it], got_rim.at[it], it, 3, me).wait_recv()

                prior = terms(
                    jnp.concatenate([got_rim[it, w] for w in range(blocks)], axis=1).astype(F32)
                )
            else:
                prior = own[at - 1]
            filtered = 0.5 * own[at][0] + 0.25 * (inside + along(prior, across.astype(F32)))
            rows = jnp.concatenate(
                [filtered[:, w * WBLK : (w + 1) * WBLK] for w in range(blocks)], axis=0
            )
            coeffs = split_mm(rows, haar_t_ref[...]) * scale
            shrunk = coeffs - jnp.clip(coeffs, -threshold, threshold)
            restored = split_mm(shrunk * scale, haar_ref[...]).astype(BF16)
            for w in range(blocks):
                piece = restored[w * total : (w + 1) * total]
                if last:
                    out_ref[at, :, w * WBLK : (w + 1) * WBLK] = piece
                else:
                    start = (w * local + at) * total
                    cur[start : start + total, :] = piece.astype(F32)

    landed(msg_a, 0, 0, send_sem)
    landed(msg_d, 0, 4, send_sem)
    for it in range(ITERS):
        landed(msg_c.at[it], it, 1, send_sem)
        landed(got_e.at[it], it, 2, send_sem)

        @pl.when(me < n - 1)
        def _():
            remote(msg_rim.at[it], got_rim.at[it], it, 3, me + 1).wait_send()


def body(n, estimate, records, dip_receiver, dip_source, delays, boat, pair):
    local, receivers, samples = estimate.shape
    total = delays.shape[0]
    record_count, local_recv, record_len = records.shape
    blocks = samples // WBLK
    cells = total * receivers * samples
    nodes = total * local
    kinds = record_count * local
    padded = max(16, kinds)
    size = blocks * nodes

    per = blocks * local * local
    vmem = pl.BlockSpec(memory_space=pltpu.VMEM)
    return pl.pallas_call(
        functools.partial(kernel, n, local, samples, float(cells)),
        out_shape=jax.ShapeDtypeStruct(estimate.shape, BF16),
        in_specs=[pl.BlockSpec(memory_space=pl.ANY)] * 7,
        out_specs=vmem,
        scratch_shapes=[
            pltpu.VMEM((size, WBLK), F32),
            pltpu.VMEM((n, per, WBLK), BF16),
            pltpu.VMEM((n, per, WBLK), BF16),
            pltpu.VMEM((n, 2 * per, WBLK), BF16),
            pltpu.VMEM((n, 2 * per, WBLK), BF16),
            pltpu.VMEM((ITERS, n, per, WBLK), BF16),
            pltpu.VMEM((ITERS, n, per, WBLK), BF16),
            pltpu.VMEM((ITERS, 1, LANES), F32),
            pltpu.VMEM((ITERS, n, 1, LANES), F32),
            pltpu.VMEM((ITERS, blocks, total, WBLK), BF16),
            pltpu.VMEM((ITERS, blocks, total, WBLK), BF16),
            pltpu.VMEM(estimate.shape, BF16),
            pltpu.VMEM(records.shape, BF16),
            pltpu.VMEM(estimate.shape, BF16),
            pltpu.VMEM(estimate.shape, BF16),
            pltpu.VMEM((1, total), jnp.int32),
            pltpu.VMEM((1, total), jnp.int32),
            pltpu.VMEM((1, total), jnp.int32),
            pltpu.VMEM((size, size), BF16),
            pltpu.VMEM((size, size), BF16),
            pltpu.VMEM((size, size), BF16),
            pltpu.VMEM((size, size), BF16),
            pltpu.VMEM((WBLK, WBLK), BF16),
            pltpu.VMEM((WBLK, WBLK), BF16),
            pltpu.VMEM((kinds, record_len), F32),
            pltpu.VMEM((nodes, LANES), jnp.int32),
            pltpu.VMEM((padded, nodes), BF16),
            pltpu.VMEM((nodes, 2 * kinds), BF16),
            pltpu.VMEM((size, size), BF16),
            pltpu.VMEM((size, size), BF16),
            pltpu.VMEM((2, size, WBLK), BF16),
            pltpu.SemaphoreType.DMA((ITERS, 5)),
            pltpu.SemaphoreType.DMA((ITERS, 5)),
            pltpu.SemaphoreType.DMA((7,)),
        ],
        compiler_params=pltpu.CompilerParams(
            collective_id=0, has_side_effects=True, vmem_limit_bytes=60 * 1024 * 1024
        ),
    )(
        estimate, records, dip_receiver, dip_source,
        delays.reshape(1, total), boat.reshape(1, total), pair.reshape(1, total),
    )


def solution(mesh):
    return jax.shard_map(
        functools.partial(body, mesh.shape["src"]),
        mesh=mesh,
        in_specs=(
            P(("parts", "src"), None, None),
            P("parts", "src", None),
            P(("parts", "src"), None, None),
            P(("parts", "src"), None, None),
            P("parts"),
            P("parts"),
            P("parts"),
        ),
        out_specs=P(("parts", "src"), None, None),
        check_vma=False,
    )
```

```python
import functools
import math

import jax
import jax.numpy as jnp
from jax import lax
from jax.experimental import pallas as pl
from jax.experimental.pallas import tpu as pltpu
from jax.sharding import PartitionSpec as P

WBLK = 256
ITERS = 2
LANES = 128

STEP_SIZE = 0.0625
SHRINK_RATIO = 0.3

F32 = jnp.float32
BF16 = jnp.bfloat16


def one_hot(ref, column_of):
    wanted = column_of(lax.broadcasted_iota(jnp.int32, (ref.shape[0], 1), 0))
    column = lax.broadcasted_iota(jnp.int32, ref.shape, 1)
    ref[...] = jnp.where(column == wanted, 1.0, 0.0).astype(BF16)


def order_maps(n, local, blocks):
    total = n * local

    def slab_of_message(i):
        j, sl = i % local, i // local % local
        w, d = i // (local * local) % blocks, i // (local * local * blocks)
        return ((w * local + sl) * n + d) * local + j

    def message_of_slab(i):
        j, d = i % local, i // local % n
        sl, w = i // total % local, i // (total * local)
        return ((d * blocks + w) * local + sl) * local + j

    def message_of_node(i):
        sl, d = i % local, i // local % n
        j, w = i // total % local, i // (total * local)
        return ((d * blocks + w) * local + sl) * local + j

    def node_of_message(i):
        j, sl = i % local, i // local % local
        w, d = i // (local * local) % blocks, i // (local * local * blocks)
        return ((w * local + j) * n + d) * local + sl

    return slab_of_message, message_of_slab, message_of_node, node_of_message


def haar_supports(index):
    support = jnp.full(index.shape, WBLK, jnp.int32)
    first = jnp.ones(index.shape, jnp.int32)
    level = 2
    while level < WBLK:
        support = jnp.where(index >= level, WBLK // level, support)
        first = jnp.where(index >= level, level, first)
        level *= 2
    start = jnp.where(index == 0, 0, (index - first) * support)
    middle = jnp.where(index == 0, WBLK, start + support // 2)
    return start, middle, start + support


def haar_signs(ref, coefficient_axis):
    shape = (WBLK, 1) if coefficient_axis == 0 else (1, WBLK)
    start, middle, end = haar_supports(lax.broadcasted_iota(jnp.int32, shape, coefficient_axis))
    time = lax.broadcasted_iota(jnp.int32, (WBLK, WBLK), 1 - coefficient_axis)
    inside = jnp.where((time >= start) & (time < middle), 1.0, 0.0)
    ref[...] = (inside - jnp.where((time >= middle) & (time < end), 1.0, 0.0)).astype(BF16)


def haar_scales():
    index = lax.broadcasted_iota(jnp.int32, (1, WBLK), 1)
    scale = jnp.full(index.shape, 1.0 / math.sqrt(WBLK), F32)
    level = 2
    while level < WBLK:
        scale = jnp.where(index >= level, math.sqrt(level / WBLK), scale)
        level *= 2
    return scale


def mm(a, b):
    return jnp.dot(a, b, preferred_element_type=F32)


def split_mm(a, b):
    high = a.astype(BF16)
    low = (a - high.astype(F32)).astype(BF16)
    return mm(high, b) + mm(low, b)


def turned(chunk, index):
    return jnp.take_along_axis(chunk, index, axis=1, mode="promise_in_bounds")


def by_row(values, rows):
    shape = (rows, values.shape[1])
    wanted = lax.broadcasted_iota(jnp.int32, shape, 0) % values.shape[1]
    lane = lax.broadcasted_iota(jnp.int32, shape, 1)
    return jnp.sum(jnp.where(lane == wanted, values, 0), axis=1, keepdims=True)


def prepare(
    local, total, blocks, me, rec_in, delays_ref, boat_ref, pair_ref,
    rec_ref, delay_ref, onto_ref, back_ref, swap_ref, swap_msg_ref,
):
    nodes = total * local
    kinds = rec_in.shape[0] * local
    for b in range(rec_in.shape[0]):
        rec_ref[b * local : (b + 1) * local, :] = rec_in[b].astype(F32)
    delay_ref[...] = jnp.broadcast_to(by_row(delays_ref[...], nodes), delay_ref.shape)
    own = lax.broadcasted_iota(jnp.int32, (nodes, 1), 0) // total
    kind = by_row(boat_ref[...], nodes) * local + own
    column = lax.broadcasted_iota(jnp.int32, back_ref.shape, 1) % kinds
    back_ref[...] = jnp.where(kind == column, 1.0, 0.0).astype(BF16)
    column = lax.broadcasted_iota(jnp.int32, (nodes, onto_ref.shape[0]), 1)
    onto_ref[...] = jnp.where(kind == column, 1.0, 0.0).T.astype(BF16)
    pairs = pair_ref[...]
    partner = by_row(pairs, total)
    partner_msg = partner // local * (blocks * local * local) + partner % local
    lane = lax.broadcasted_iota(jnp.int32, pairs.shape, 1)
    column = lax.broadcasted_iota(jnp.int32, (total, swap_ref.shape[1]), 1)
    for sl in range(local):
        first = me * local
        mate = jnp.sum(jnp.where(lane == first + sl, pairs - first, 0), axis=1, keepdims=True)
        for w in range(blocks):
            start = (w * local + sl) * total
            swap_ref[start : start + total, :] = jnp.where(
                column == partner + (mate + w * local) * total, 1.0, 0.0
            ).astype(BF16)
            swap_msg_ref[start : start + total, :] = jnp.where(
                column == partner_msg + (mate + w * local) * local, 1.0, 0.0
            ).astype(BF16)


def by_slab(rows, at, local, total):
    count = rows.shape[0] // (local * total)
    return jnp.concatenate(
        [rows[(w * local + at) * total : (w * local + at + 1) * total] for w in range(count)],
        axis=1,
    )


def terms(value):
    samples = value.shape[1]
    time = lax.broadcasted_iota(jnp.int32, value.shape, 1)
    before = jnp.where(time == 0, 0.0, pltpu.roll(value, 1, axis=1))
    after = jnp.where(time == samples - 1, 0.0, pltpu.roll(value, samples - 1, axis=1))
    return value, 0.5 * (before - after), 0.5 * (before + after) - value


def below(value):
    row = lax.broadcasted_iota(jnp.int32, value.shape, 0)
    return jnp.where(row == 0, 0.0, pltpu.roll(value, 1, axis=0))


def along(parts, dip):
    value, slope, bend = parts
    return value + dip * (slope + dip * bend)


def kernel(
    n, local, samples, cells,
    est_hbm, rec_hbm, dipr_hbm, dips_hbm, delays_hbm, boat_hbm, pair_hbm,
    out_ref,
    cur, msg_a, got_a, msg_d, got_d, msg_c, got_c, msg_e, got_e, msg_rim, got_rim,
    est_ref, rec_in, dipr_ref, dips_ref, delays_ref, boat_ref, pair_ref,
    to_msg_ref, from_msg_ref, to_node_ref, from_node_ref, haar_t_ref, haar_ref,
    rec_ref, delay_ref, onto_ref, back_ref, swap_ref, swap_msg_ref, dip_node,
    send_sem, recv_sem, load_sem,
):
    me = lax.axis_index("src")
    total = n * local
    blocks = samples // WBLK
    chunks = samples // LANES
    per = blocks * local * local
    nodes = total * local

    barrier = pltpu.get_barrier_semaphore()

    bits = [me // 2**i % 2 for i in range(n.bit_length() - 1)]

    def partner_at(k):
        return sum((1 - bit if k >> i & 1 else bit) * 2**i for i, bit in enumerate(bits))

    for k in reversed(range(1, n)):
        pl.semaphore_signal(
            barrier, inc=1, device_id={"src": partner_at(k)},
            device_id_type=pl.DeviceIdType.MESH,
        )

    loads = [
        pltpu.make_async_copy(src, dst, load_sem.at[i])
        for i, (src, dst) in enumerate(
            [
                (est_hbm, est_ref), (dipr_hbm, dipr_ref), (dips_hbm, dips_ref),
                (delays_hbm, delays_ref), (boat_hbm, boat_ref), (pair_hbm, pair_ref),
                (rec_hbm, rec_in),
            ]
        )
    ]
    for load in loads:
        load.start()

    def remote(src, dst, it, kind, target):
        return pltpu.make_async_remote_copy(
            src_ref=src, dst_ref=dst,
            send_sem=send_sem.at[it, kind], recv_sem=recv_sem.at[it, kind],
            device_id={"src": target}, device_id_type=pl.DeviceIdType.MESH,
        )

    def landed(buf, it, kind, sems):
        whole = buf.at[pl.ds(0, n - 1)]
        pltpu.make_async_copy(whole, whole, sems.at[it, kind]).wait()

    slab_of_message, message_of_slab, message_of_node, node_of_message = order_maps(
        n, local, blocks
    )
    one_hot(to_msg_ref, slab_of_message)

    def packed(ref):
        rows = jnp.concatenate(
            [
                ref[sl, :, w * WBLK : (w + 1) * WBLK]
                for w in range(blocks)
                for sl in range(local)
            ],
            axis=0,
        )
        return mm(to_msg_ref[...], rows).astype(BF16).reshape(n, per, WBLK)

    loads[0].wait()
    msg_a[...] = packed(est_ref)
    got_a[me] = msg_a[me]
    loads[1].wait()
    loads[2].wait()
    msg_d[:, :per, :] = packed(dipr_ref)
    msg_d[:, per:, :] = packed(dips_ref)
    got_d[me] = msg_d[me]
    pl.semaphore_wait(barrier, n - 1)

    for k in reversed(range(1, n)):
        target = partner_at(k)
        remote(msg_a.at[target], got_a.at[me], 0, 0, target).start()

    for load in loads[3:]:
        load.wait()
    one_hot(to_node_ref, message_of_node)
    prepare(
        local, total, blocks, me, rec_in, delays_ref, boat_ref, pair_ref,
        rec_ref, delay_ref, onto_ref, back_ref, swap_ref, swap_msg_ref,
    )
    one_hot(from_node_ref, node_of_message)
    one_hot(from_msg_ref, message_of_slab)
    haar_signs(haar_t_ref, 1)
    haar_signs(haar_ref, 0)
    scale = haar_scales()

    landed(msg_a, 0, 0, send_sem)

    for k in reversed(range(1, n)):
        target = partner_at(k)
        remote(msg_d.at[target], got_d.at[me], 0, 4, target).start()

    landed(got_a, 0, 0, recv_sem)
    cur[...] = mm(to_node_ref[...], got_a[...].reshape(n * per, WBLK))

    for it in range(ITERS):
        last = it == ITERS - 1
        delay = delay_ref[...]
        lane = lax.broadcasted_iota(jnp.int32, delay.shape, 1)
        later_index = (lane - delay) & (LANES - 1)
        earlier_index = (lane + delay) & (LANES - 1)
        from_before = lane < delay
        from_same = lane < LANES - delay
        nothing = jnp.zeros(delay.shape, F32)
        wide = [
            cur[(c // 2) * nodes : (c // 2 + 1) * nodes, (c % 2) * LANES : (c % 2 + 1) * LANES]
            for c in range(chunks)
        ]
        moved = [turned(chunk, later_index) for chunk in wide]
        placed = [
            jnp.where(
                from_before,
                moved[c - 1] if c > 0 else nothing,
                moved[c] if c < chunks else nothing,
            ).astype(BF16)
            for c in range(chunks + 1)
        ]
        predicted = mm(onto_ref[...], jnp.concatenate(placed, axis=1))
        residual = rec_ref[...] - predicted[: rec_ref.shape[0]]
        high = residual.astype(BF16).astype(F32)
        pieces = jnp.concatenate([high, residual - high], axis=0).astype(BF16)
        picked = mm(back_ref[...], pieces)
        moved = [
            turned(picked[:, c * LANES : (c + 1) * LANES], earlier_index) for c in range(chunks + 1)
        ]
        update = [
            (wide[c] + STEP_SIZE * jnp.where(from_same, moved[c], moved[c + 1])).astype(BF16)
            for c in range(chunks)
        ]
        update_rows = jnp.concatenate(
            [jnp.concatenate(update[2 * w : 2 * w + 2], axis=1) for w in range(blocks)], axis=0
        )
        msg_c[it] = mm(from_node_ref[...], update_rows).astype(BF16).reshape(n, per, WBLK)

        for k in reversed(range(1, n)):
            target = partner_at(k)
            remote(msg_c.at[it, target], got_c.at[it, me], it, 1, target).start()

        square = nothing
        for piece in update:
            piece = piece.astype(F32)
            square = square + piece * piece
        msg_e[it] = jnp.sum(square, axis=0, keepdims=True)

        for k in reversed(range(1, n)):
            target = partner_at(k)
            remote(msg_e.at[it], got_e.at[it, me], it, 2, target).start()

        got_e[it, me] = msg_e[it]
        got_c[it, me] = msg_c[it, me]

        if not last:
            landed(got_d, 0, 4, recv_sem)
            for i in range(2):
                rows = got_d[:, i * per : (i + 1) * per, :].reshape(n * per, WBLK)
                dip_node[i] = mm(to_node_ref[...], rows).astype(BF16)
            kept = update_rows.astype(F32)
        else:
            kept = mm(swap_ref[...], update_rows)
        arrange = from_msg_ref if last else swap_msg_ref
        landed(got_c.at[it], it, 1, recv_sem)
        symmetric = (
            0.5 * (mm(arrange[...], got_c[it].reshape(n * per, WBLK)) + kept)
        ).astype(BF16)
        for w in range(blocks):
            start = (w * local + local - 1) * total
            msg_rim[it, w] = symmetric[start : start + total]

        @pl.when(me < n - 1)
        def _():
            remote(msg_rim.at[it], got_rim.at[it], it, 3, me + 1).start()

        @pl.when(me == 0)
        def _():
            got_rim[it] = jnp.zeros(got_rim.shape[1:], BF16)

        own = [terms(by_slab(symmetric, at, local, total).astype(F32)) for at in range(local)]

        landed(got_e.at[it], it, 2, recv_sem)
        energy = jnp.sum(got_e[it].reshape(n, LANES))
        threshold = SHRINK_RATIO * jnp.sqrt(jnp.full((1, WBLK), energy) / cells + 1e-6)

        for at in reversed(range(local)):
            if last:
                within, across = dipr_ref[at], dips_ref[at]
            else:
                within = by_slab(dip_node[1], at, local, total)
                across = by_slab(dip_node[0], at, local, total)
            inside = along([below(part) for part in own[at]], within.astype(F32))
            if at == 0:
                @pl.when(me > 0)
                def _():
                    remote(msg_rim.at[it], got_rim.at[it], it, 3, me).wait_recv()

                prior = terms(
                    jnp.concatenate([got_rim[it, w] for w in range(blocks)], axis=1).astype(F32)
                )
            else:
                prior = own[at - 1]
            filtered = 0.5 * own[at][0] + 0.25 * (inside + along(prior, across.astype(F32)))
            rows = jnp.concatenate(
                [filtered[:, w * WBLK : (w + 1) * WBLK] for w in range(blocks)], axis=0
            )
            coeffs = split_mm(rows, haar_t_ref[...]) * scale
            shrunk = coeffs - jnp.clip(coeffs, -threshold, threshold)
            restored = split_mm(shrunk * scale, haar_ref[...]).astype(BF16)
            for w in range(blocks):
                piece = restored[w * total : (w + 1) * total]
                if last:
                    out_ref[at, :, w * WBLK : (w + 1) * WBLK] = piece
                else:
                    start = (w * local + at) * total
                    cur[start : start + total, :] = piece.astype(F32)

    landed(msg_d, 0, 4, send_sem)
    for it in range(ITERS):
        landed(msg_c.at[it], it, 1, send_sem)
        landed(got_e.at[it], it, 2, send_sem)

        @pl.when(me < n - 1)
        def _():
            remote(msg_rim.at[it], got_rim.at[it], it, 3, me + 1).wait_send()


def body(n, estimate, records, dip_receiver, dip_source, delays, boat, pair):
    local, receivers, samples = estimate.shape
    total = delays.shape[0]
    record_count, local_recv, record_len = records.shape
    blocks = samples // WBLK
    cells = total * receivers * samples
    nodes = total * local
    kinds = record_count * local
    padded = max(16, kinds)
    size = blocks * nodes

    per = blocks * local * local
    vmem = pl.BlockSpec(memory_space=pltpu.VMEM)
    return pl.pallas_call(
        functools.partial(kernel, n, local, samples, float(cells)),
        out_shape=jax.ShapeDtypeStruct(estimate.shape, BF16),
        in_specs=[pl.BlockSpec(memory_space=pl.ANY)] * 7,
        out_specs=vmem,
        scratch_shapes=[
            pltpu.VMEM((size, WBLK), F32),
            pltpu.VMEM((n, per, WBLK), BF16),
            pltpu.VMEM((n, per, WBLK), BF16),
            pltpu.VMEM((n, 2 * per, WBLK), BF16),
            pltpu.VMEM((n, 2 * per, WBLK), BF16),
            pltpu.VMEM((ITERS, n, per, WBLK), BF16),
            pltpu.VMEM((ITERS, n, per, WBLK), BF16),
            pltpu.VMEM((ITERS, 1, LANES), F32),
            pltpu.VMEM((ITERS, n, 1, LANES), F32),
            pltpu.VMEM((ITERS, blocks, total, WBLK), BF16),
            pltpu.VMEM((ITERS, blocks, total, WBLK), BF16),
            pltpu.VMEM(estimate.shape, BF16),
            pltpu.VMEM(records.shape, BF16),
            pltpu.VMEM(estimate.shape, BF16),
            pltpu.VMEM(estimate.shape, BF16),
            pltpu.VMEM((1, total), jnp.int32),
            pltpu.VMEM((1, total), jnp.int32),
            pltpu.VMEM((1, total), jnp.int32),
            pltpu.VMEM((size, size), BF16),
            pltpu.VMEM((size, size), BF16),
            pltpu.VMEM((size, size), BF16),
            pltpu.VMEM((size, size), BF16),
            pltpu.VMEM((WBLK, WBLK), BF16),
            pltpu.VMEM((WBLK, WBLK), BF16),
            pltpu.VMEM((kinds, record_len), F32),
            pltpu.VMEM((nodes, LANES), jnp.int32),
            pltpu.VMEM((padded, nodes), BF16),
            pltpu.VMEM((nodes, 2 * kinds), BF16),
            pltpu.VMEM((size, size), BF16),
            pltpu.VMEM((size, size), BF16),
            pltpu.VMEM((2, size, WBLK), BF16),
            pltpu.SemaphoreType.DMA((ITERS, 5)),
            pltpu.SemaphoreType.DMA((ITERS, 5)),
            pltpu.SemaphoreType.DMA((7,)),
        ],
        compiler_params=pltpu.CompilerParams(
            collective_id=0, has_side_effects=True, vmem_limit_bytes=60 * 1024 * 1024
        ),
    )(
        estimate, records, dip_receiver, dip_source,
        delays.reshape(1, total), boat.reshape(1, total), pair.reshape(1, total),
    )


def solution(mesh):
    return jax.shard_map(
        functools.partial(body, mesh.shape["src"]),
        mesh=mesh,
        in_specs=(
            P(("parts", "src"), None, None),
            P("parts", "src", None),
            P(("parts", "src"), None, None),
            P(("parts", "src"), None, None),
            P("parts"),
            P("parts"),
            P("parts"),
        ),
        out_specs=P(("parts", "src"), None, None),
        check_vma=False,
    )
```

```python
import functools
import math

import jax
import jax.numpy as jnp
from jax import lax
from jax.experimental import pallas as pl
from jax.experimental.pallas import tpu as pltpu
from jax.sharding import PartitionSpec as P

WBLK = 256
ITERS = 2
LANES = 128

STEP_SIZE = 0.0625
SHRINK_RATIO = 0.3

F32 = jnp.float32
BF16 = jnp.bfloat16


def one_hot(ref, column_of):
    wanted = column_of(lax.broadcasted_iota(jnp.int32, (ref.shape[0], 1), 0))
    column = lax.broadcasted_iota(jnp.int32, ref.shape, 1)
    ref[...] = jnp.where(column == wanted, 1.0, 0.0).astype(BF16)


def order_maps(n, local, blocks):
    total = n * local

    def slab_of_message(i):
        j, sl = i % local, i // local % local
        w, d = i // (local * local) % blocks, i // (local * local * blocks)
        return ((w * local + sl) * n + d) * local + j

    def message_of_slab(i):
        j, d = i % local, i // local % n
        sl, w = i // total % local, i // (total * local)
        return ((d * blocks + w) * local + sl) * local + j

    def message_of_node(i):
        sl, d = i % local, i // local % n
        j, w = i // total % local, i // (total * local)
        return ((d * blocks + w) * local + sl) * local + j

    def node_of_message(i):
        j, sl = i % local, i // local % local
        w, d = i // (local * local) % blocks, i // (local * local * blocks)
        return ((w * local + j) * n + d) * local + sl

    return slab_of_message, message_of_slab, message_of_node, node_of_message


def haar_supports(index):
    support = jnp.full(index.shape, WBLK, jnp.int32)
    first = jnp.ones(index.shape, jnp.int32)
    level = 2
    while level < WBLK:
        support = jnp.where(index >= level, WBLK // level, support)
        first = jnp.where(index >= level, level, first)
        level *= 2
    start = jnp.where(index == 0, 0, (index - first) * support)
    middle = jnp.where(index == 0, WBLK, start + support // 2)
    return start, middle, start + support


def haar_signs(ref, coefficient_axis):
    shape = (WBLK, 1) if coefficient_axis == 0 else (1, WBLK)
    start, middle, end = haar_supports(lax.broadcasted_iota(jnp.int32, shape, coefficient_axis))
    time = lax.broadcasted_iota(jnp.int32, (WBLK, WBLK), 1 - coefficient_axis)
    inside = jnp.where((time >= start) & (time < middle), 1.0, 0.0)
    ref[...] = (inside - jnp.where((time >= middle) & (time < end), 1.0, 0.0)).astype(BF16)


def haar_scales():
    index = lax.broadcasted_iota(jnp.int32, (1, WBLK), 1)
    scale = jnp.full(index.shape, 1.0 / math.sqrt(WBLK), F32)
    level = 2
    while level < WBLK:
        scale = jnp.where(index >= level, math.sqrt(level / WBLK), scale)
        level *= 2
    return scale


def mm(a, b):
    return jnp.dot(a, b, preferred_element_type=F32)


def split_mm(a, b):
    high = a.astype(BF16)
    low = (a - high.astype(F32)).astype(BF16)
    return mm(high, b) + mm(low, b)


def turned(chunk, index):
    return jnp.take_along_axis(chunk, index, axis=1, mode="promise_in_bounds")


def by_row(values, rows):
    shape = (rows, values.shape[1])
    wanted = lax.broadcasted_iota(jnp.int32, shape, 0) % values.shape[1]
    lane = lax.broadcasted_iota(jnp.int32, shape, 1)
    return jnp.sum(jnp.where(lane == wanted, values, 0), axis=1, keepdims=True)


def prepare(
    local, total, blocks, me, rec_in, delays_ref, boat_ref, pair_ref,
    rec_ref, delay_ref, onto_ref, back_ref, swap_ref, swap_msg_ref,
):
    nodes = total * local
    kinds = rec_in.shape[0] * local
    for b in range(rec_in.shape[0]):
        rec_ref[b * local : (b + 1) * local, :] = rec_in[b].astype(F32)
    delay_ref[...] = jnp.broadcast_to(by_row(delays_ref[...], nodes), delay_ref.shape)
    own = lax.broadcasted_iota(jnp.int32, (nodes, 1), 0) // total
    kind = by_row(boat_ref[...], nodes) * local + own
    column = lax.broadcasted_iota(jnp.int32, back_ref.shape, 1) % kinds
    back_ref[...] = jnp.where(kind == column, 1.0, 0.0).astype(BF16)
    column = lax.broadcasted_iota(jnp.int32, (nodes, onto_ref.shape[0]), 1)
    onto_ref[...] = jnp.where(kind == column, 1.0, 0.0).T.astype(BF16)
    pairs = pair_ref[...]
    partner = by_row(pairs, total)
    partner_msg = partner // local * (blocks * local * local) + partner % local
    lane = lax.broadcasted_iota(jnp.int32, pairs.shape, 1)
    column = lax.broadcasted_iota(jnp.int32, (total, swap_ref.shape[1]), 1)
    for sl in range(local):
        first = me * local
        mate = jnp.sum(jnp.where(lane == first + sl, pairs - first, 0), axis=1, keepdims=True)
        for w in range(blocks):
            start = (w * local + sl) * total
            swap_ref[start : start + total, :] = jnp.where(
                column == partner + (mate + w * local) * total, 1.0, 0.0
            ).astype(BF16)
            swap_msg_ref[start : start + total, :] = jnp.where(
                column == partner_msg + (mate + w * local) * local, 1.0, 0.0
            ).astype(BF16)


def by_slab(rows, at, local, total):
    count = rows.shape[0] // (local * total)
    return jnp.concatenate(
        [rows[(w * local + at) * total : (w * local + at + 1) * total] for w in range(count)],
        axis=1,
    )


def terms(value):
    samples = value.shape[1]
    time = lax.broadcasted_iota(jnp.int32, value.shape, 1)
    before = jnp.where(time == 0, 0.0, pltpu.roll(value, 1, axis=1))
    after = jnp.where(time == samples - 1, 0.0, pltpu.roll(value, samples - 1, axis=1))
    return value, 0.5 * (before - after), 0.5 * (before + after) - value


def below(value):
    row = lax.broadcasted_iota(jnp.int32, value.shape, 0)
    return jnp.where(row == 0, 0.0, pltpu.roll(value, 1, axis=0))


def along(parts, dip):
    value, slope, bend = parts
    return value + dip * (slope + dip * bend)


def kernel(
    n, local, samples, cells,
    est_hbm, rec_hbm, dipr_hbm, dips_hbm, delays_hbm, boat_hbm, pair_hbm,
    out_ref,
    cur, msg_a, got_a, msg_d, got_d, msg_c, got_c, msg_e, got_e, msg_rim, got_rim,
    est_ref, rec_in, dipr_ref, dips_ref, delays_ref, boat_ref, pair_ref,
    to_msg_ref, from_msg_ref, to_node_ref, from_node_ref, haar_t_ref, haar_ref,
    rec_ref, delay_ref, onto_ref, back_ref, swap_ref, swap_msg_ref, dip_node,
    send_sem, recv_sem, load_sem,
):
    me = lax.axis_index("src")
    total = n * local
    blocks = samples // WBLK
    chunks = samples // LANES
    per = blocks * local * local
    nodes = total * local

    barrier = pltpu.get_barrier_semaphore()

    bits = [me // 2**i % 2 for i in range(n.bit_length() - 1)]

    def partner_at(k):
        return sum((1 - bit if k >> i & 1 else bit) * 2**i for i, bit in enumerate(bits))

    for k in reversed(range(1, n)):
        pl.semaphore_signal(
            barrier, inc=1, device_id={"src": partner_at(k)},
            device_id_type=pl.DeviceIdType.MESH,
        )

    loads = [
        pltpu.make_async_copy(src, dst, load_sem.at[i])
        for i, (src, dst) in enumerate(
            [
                (est_hbm, est_ref), (dipr_hbm, dipr_ref), (dips_hbm, dips_ref),
                (delays_hbm, delays_ref), (boat_hbm, boat_ref), (pair_hbm, pair_ref),
                (rec_hbm, rec_in),
            ]
        )
    ]
    for load in loads:
        load.start()

    def remote(src, dst, it, kind, target):
        return pltpu.make_async_remote_copy(
            src_ref=src, dst_ref=dst,
            send_sem=send_sem.at[it, kind], recv_sem=recv_sem.at[it, kind],
            device_id={"src": target}, device_id_type=pl.DeviceIdType.MESH,
        )

    def landed(buf, it, kind, sems):
        whole = buf.at[pl.ds(0, n - 1)]
        pltpu.make_async_copy(whole, whole, sems.at[it, kind]).wait()

    slab_of_message, message_of_slab, message_of_node, node_of_message = order_maps(
        n, local, blocks
    )
    one_hot(to_msg_ref, slab_of_message)

    def packed(ref):
        rows = jnp.concatenate(
            [
                ref[sl, :, w * WBLK : (w + 1) * WBLK]
                for w in range(blocks)
                for sl in range(local)
            ],
            axis=0,
        )
        return mm(to_msg_ref[...], rows).astype(BF16).reshape(n, per, WBLK)

    loads[0].wait()
    msg_a[...] = packed(est_ref)
    got_a[me] = msg_a[me]
    loads[1].wait()
    loads[2].wait()
    msg_d[:, :per, :] = packed(dipr_ref)
    msg_d[:, per:, :] = packed(dips_ref)
    got_d[me] = msg_d[me]
    pl.semaphore_wait(barrier, n - 1)

    for k in reversed(range(1, n)):
        target = partner_at(k)
        remote(msg_a.at[target], got_a.at[me], 0, 0, target).start()

    for load in loads[3:]:
        load.wait()
    one_hot(to_node_ref, message_of_node)
    prepare(
        local, total, blocks, me, rec_in, delays_ref, boat_ref, pair_ref,
        rec_ref, delay_ref, onto_ref, back_ref, swap_ref, swap_msg_ref,
    )
    one_hot(from_node_ref, node_of_message)
    one_hot(from_msg_ref, message_of_slab)
    haar_signs(haar_t_ref, 1)
    haar_signs(haar_ref, 0)
    scale = haar_scales()

    landed(msg_a, 0, 0, send_sem)

    for k in reversed(range(1, n)):
        target = partner_at(k)
        remote(msg_d.at[target], got_d.at[me], 0, 4, target).start()

    landed(got_a, 0, 0, recv_sem)
    cur[...] = mm(to_node_ref[...], got_a[...].reshape(n * per, WBLK))

    for it in range(ITERS):
        last = it == ITERS - 1
        delay = delay_ref[...]
        lane = lax.broadcasted_iota(jnp.int32, delay.shape, 1)
        later_index = (lane - delay) & (LANES - 1)
        earlier_index = (lane + delay) & (LANES - 1)
        from_before = lane < delay
        from_same = lane < LANES - delay
        nothing = jnp.zeros(delay.shape, F32)
        wide = [
            cur[(c // 2) * nodes : (c // 2 + 1) * nodes, (c % 2) * LANES : (c % 2 + 1) * LANES]
            for c in range(chunks)
        ]
        moved = [turned(chunk, later_index) for chunk in wide]
        placed = [
            jnp.where(
                from_before,
                moved[c - 1] if c > 0 else nothing,
                moved[c] if c < chunks else nothing,
            ).astype(BF16)
            for c in range(chunks + 1)
        ]
        predicted = mm(onto_ref[...], jnp.concatenate(placed, axis=1))
        residual = rec_ref[...] - predicted[: rec_ref.shape[0]]
        high = residual.astype(BF16).astype(F32)
        pieces = jnp.concatenate([high, residual - high], axis=0).astype(BF16)
        picked = mm(back_ref[...], pieces)
        moved = [
            turned(picked[:, c * LANES : (c + 1) * LANES], earlier_index) for c in range(chunks + 1)
        ]
        update = [
            (wide[c] + STEP_SIZE * jnp.where(from_same, moved[c], moved[c + 1])).astype(BF16)
            for c in range(chunks)
        ]
        update_rows = jnp.concatenate(
            [jnp.concatenate(update[2 * w : 2 * w + 2], axis=1) for w in range(blocks)], axis=0
        )
        msg_c[it] = mm(from_node_ref[...], update_rows).astype(BF16).reshape(n, per, WBLK)

        for k in reversed(range(1, n)):
            target = partner_at(k)
            remote(msg_c.at[it, target], got_c.at[it, me], it, 1, target).start()

        square = nothing
        for piece in update:
            piece = piece.astype(F32)
            square = square + piece * piece
        msg_e[it] = jnp.sum(square, axis=0, keepdims=True)

        for k in reversed(range(1, n)):
            target = partner_at(k)
            remote(msg_e.at[it], got_e.at[it, me], it, 2, target).start()

        got_e[it, me] = msg_e[it]
        got_c[it, me] = msg_c[it, me]

        if not last:
            landed(got_d, 0, 4, recv_sem)
            for i in range(2):
                rows = got_d[:, i * per : (i + 1) * per, :].reshape(n * per, WBLK)
                dip_node[i] = mm(to_node_ref[...], rows).astype(BF16)
            kept = update_rows.astype(F32)
        else:
            kept = mm(swap_ref[...], update_rows)
        arrange = from_msg_ref if last else swap_msg_ref
        landed(got_c.at[it], it, 1, recv_sem)
        arrived = got_c[it].reshape(n * per, WBLK)

        def symmetric(at):
            starts = [(w * local + at) * total for w in range(blocks)]
            table = jnp.concatenate([arrange[i : i + total, :] for i in starts], axis=0)
            here = jnp.concatenate([kept[i : i + total] for i in starts], axis=0)
            return (0.5 * (mm(table, arrived) + here)).astype(BF16)

        edge = symmetric(local - 1)
        msg_rim[it] = edge.reshape(blocks, total, WBLK)

        @pl.when(me < n - 1)
        def _():
            remote(msg_rim.at[it], got_rim.at[it], it, 3, me + 1).start()

        @pl.when(me == 0)
        def _():
            got_rim[it] = jnp.zeros(got_rim.shape[1:], BF16)

        slabs = [symmetric(at) for at in range(local - 1)] + [edge]
        own = [terms(by_slab(slab, 0, 1, total).astype(F32)) for slab in slabs]

        landed(got_e.at[it], it, 2, recv_sem)
        energy = jnp.sum(got_e[it].reshape(n, LANES))
        threshold = SHRINK_RATIO * jnp.sqrt(jnp.full((1, WBLK), energy) / cells + 1e-6)

        for at in reversed(range(local)):
            if last:
                within, across = dipr_ref[at], dips_ref[at]
            else:
                within = by_slab(dip_node[1], at, local, total)
                across = by_slab(dip_node[0], at, local, total)
            inside = along([below(part) for part in own[at]], within.astype(F32))
            if at == 0:
                @pl.when(me > 0)
                def _():
                    remote(msg_rim.at[it], got_rim.at[it], it, 3, me).wait_recv()

                prior = terms(
                    jnp.concatenate([got_rim[it, w] for w in range(blocks)], axis=1).astype(F32)
                )
            else:
                prior = own[at - 1]
            filtered = 0.5 * own[at][0] + 0.25 * (inside + along(prior, across.astype(F32)))
            rows = jnp.concatenate(
                [filtered[:, w * WBLK : (w + 1) * WBLK] for w in range(blocks)], axis=0
            )
            coeffs = split_mm(rows, haar_t_ref[...]) * scale
            shrunk = coeffs - jnp.clip(coeffs, -threshold, threshold)
            restored = split_mm(shrunk * scale, haar_ref[...]).astype(BF16)
            for w in range(blocks):
                piece = restored[w * total : (w + 1) * total]
                if last:
                    out_ref[at, :, w * WBLK : (w + 1) * WBLK] = piece
                else:
                    start = (w * local + at) * total
                    cur[start : start + total, :] = piece.astype(F32)

    landed(msg_d, 0, 4, send_sem)
    for it in range(ITERS):
        landed(msg_c.at[it], it, 1, send_sem)
        landed(got_e.at[it], it, 2, send_sem)

        @pl.when(me < n - 1)
        def _():
            remote(msg_rim.at[it], got_rim.at[it], it, 3, me + 1).wait_send()


def body(n, estimate, records, dip_receiver, dip_source, delays, boat, pair):
    local, receivers, samples = estimate.shape
    total = delays.shape[0]
    record_count, local_recv, record_len = records.shape
    blocks = samples // WBLK
    cells = total * receivers * samples
    nodes = total * local
    kinds = record_count * local
    padded = max(16, kinds)
    size = blocks * nodes

    per = blocks * local * local
    vmem = pl.BlockSpec(memory_space=pltpu.VMEM)
    return pl.pallas_call(
        functools.partial(kernel, n, local, samples, float(cells)),
        out_shape=jax.ShapeDtypeStruct(estimate.shape, BF16),
        in_specs=[pl.BlockSpec(memory_space=pl.ANY)] * 7,
        out_specs=vmem,
        scratch_shapes=[
            pltpu.VMEM((size, WBLK), F32),
            pltpu.VMEM((n, per, WBLK), BF16),
            pltpu.VMEM((n, per, WBLK), BF16),
            pltpu.VMEM((n, 2 * per, WBLK), BF16),
            pltpu.VMEM((n, 2 * per, WBLK), BF16),
            pltpu.VMEM((ITERS, n, per, WBLK), BF16),
            pltpu.VMEM((ITERS, n, per, WBLK), BF16),
            pltpu.VMEM((ITERS, 1, LANES), F32),
            pltpu.VMEM((ITERS, n, 1, LANES), F32),
            pltpu.VMEM((ITERS, blocks, total, WBLK), BF16),
            pltpu.VMEM((ITERS, blocks, total, WBLK), BF16),
            pltpu.VMEM(estimate.shape, BF16),
            pltpu.VMEM(records.shape, BF16),
            pltpu.VMEM(estimate.shape, BF16),
            pltpu.VMEM(estimate.shape, BF16),
            pltpu.VMEM((1, total), jnp.int32),
            pltpu.VMEM((1, total), jnp.int32),
            pltpu.VMEM((1, total), jnp.int32),
            pltpu.VMEM((size, size), BF16),
            pltpu.VMEM((size, size), BF16),
            pltpu.VMEM((size, size), BF16),
            pltpu.VMEM((size, size), BF16),
            pltpu.VMEM((WBLK, WBLK), BF16),
            pltpu.VMEM((WBLK, WBLK), BF16),
            pltpu.VMEM((kinds, record_len), F32),
            pltpu.VMEM((nodes, LANES), jnp.int32),
            pltpu.VMEM((padded, nodes), BF16),
            pltpu.VMEM((nodes, 2 * kinds), BF16),
            pltpu.VMEM((size, size), BF16),
            pltpu.VMEM((size, size), BF16),
            pltpu.VMEM((2, size, WBLK), BF16),
            pltpu.SemaphoreType.DMA((ITERS, 5)),
            pltpu.SemaphoreType.DMA((ITERS, 5)),
            pltpu.SemaphoreType.DMA((7,)),
        ],
        compiler_params=pltpu.CompilerParams(
            collective_id=0, has_side_effects=True, vmem_limit_bytes=60 * 1024 * 1024
        ),
    )(
        estimate, records, dip_receiver, dip_source,
        delays.reshape(1, total), boat.reshape(1, total), pair.reshape(1, total),
    )


def solution(mesh):
    return jax.shard_map(
        functools.partial(body, mesh.shape["src"]),
        mesh=mesh,
        in_specs=(
            P(("parts", "src"), None, None),
            P("parts", "src", None),
            P(("parts", "src"), None, None),
            P(("parts", "src"), None, None),
            P("parts"),
            P("parts"),
            P("parts"),
        ),
        out_specs=P(("parts", "src"), None, None),
        check_vma=False,
    )
```
